128 devices in a mesh: cube: 8 (over y_lo, z), row: 4 (over x), col: 4 (over y_hi, core).
Axes of the slice: x: 4, y: 4 (y_hi: 2, y_lo: 2; y = y_hi * 2 + y_lo), z: 4, core: 2. Of those that a mesh axis runs over, the one named last changes fastest.
Arguments:
- front_entries: float32 [8, 6144, 6144], P('cube', 'row', 'col')
- child_update: float32 [8, 3072, 3072], P('cube', 'row', 'col')
- block_map: int32 [8, 2, 24], P('cube'), may hold values from 0 to 47, as said below
Outputs:
- factored: float32 [8, 6144, 6144], P('cube', 'row', 'col')
The draws below stay inside these ranges and needn't reach their ends.
Inputs may be any that keep to these rules, and one draw needn't show every extreme that they name: `block_map`: for each front and child the 24 entries are distinct. Among the child blocks of one device (blocks t * 3072 / 512 to the next such bound) at most 2 go to parent blocks of one grid row, parent block // (6144 / 512); some go exactly 2.
All inputs are finite; a program needn't handle non-finite values.
Results may differ from the reference program's by a relative error of at most 0.0001.
Values sent between devices are 32-bit elements; how exact they have to be, the bound alone decides.
No kernel may reach another device: no remote copies, remote signals or barrier semaphores. Data moves between devices by JAX's collectives and lax.ppermute only.
A program may use at most 192 MiB of HBM per device.

```python
import math
import jax
import jax.numpy as jnp
from jax import lax

NF = 6144
NU = 3072
BLK = 128
CAP = 2
PW = 256
PANELS = 2
GROUPS = 8
N_ROW = 4


def symmetric_part(raw_values, factor):
    sym_values = (raw_values + jnp.swapaxes(raw_values, 1, 2)) * (factor / math.sqrt(2.0))
    return sym_values


def smooth_part(key_smooth, coupling, decay_rate, lowest, highest):
    amplitude = jnp.exp(jax.random.uniform(key_smooth, (GROUPS, NF), jnp.float32, math.log(lowest), math.log(highest)))
    positions = jnp.arange(NF).astype(jnp.float32)
    distance = jnp.abs(positions[:, None] - positions[None, :])
    kernel = jnp.exp(distance * math.log(decay_rate))
    return coupling * amplitude[:, :, None] * amplitude[:, None, :] * kernel[None]


def draw_front_entries(key, part):
    key = jax.random.fold_in(key, 1)
    key_raw = jax.random.fold_in(key, 0)
    key_diag = jax.random.fold_in(key, 1)
    key_smooth = jax.random.fold_in(key, 3)
    raw_values = jax.random.normal(key_raw, (GROUPS, NF, NF), jnp.float32)
    diagonal = jax.random.uniform(key_diag, (GROUPS, NF), jnp.float32, 8.0, 16.0)
    smooth = smooth_part(key_smooth, 6.0, 0.9, 0.7, 1.4)
    sym_values = symmetric_part(raw_values, 2.0 / math.sqrt(NF))
    on_diag = jnp.arange(NF)[:, None] == jnp.arange(NF)[None, :]
    return jnp.where(on_diag[None], diagonal[:, None, :], sym_values) + smooth


def draw_child_update(key, part):
    key = jax.random.fold_in(key, 2)
    key_raw = jax.random.fold_in(key, 0)
    raw_values = jax.random.normal(key_raw, (GROUPS, NU, NU), jnp.float32)
    return symmetric_part(raw_values, 2.0 / math.sqrt(NU))


def one_block_map(key):
    child_local = NU // (BLK * N_ROW)
    parent_local = NF // (BLK * N_ROW)
    key_count, key_order, key_slot = jax.random.split(key, 3)
    base_counts = jnp.minimum(CAP, jnp.maximum(0, child_local - CAP * jnp.arange(N_ROW)))
    orders = jax.vmap(lambda single: jax.random.permutation(single, N_ROW))(jax.random.split(key_count, N_ROW))
    counts = base_counts[orders]

    def sequence(count_row, single):
        listed = jnp.repeat(jnp.arange(N_ROW), count_row, total_repeat_length=child_local)
        return listed[jax.random.permutation(single, child_local)]
    targets = jax.vmap(sequence)(counts, jax.random.split(key_order, N_ROW))
    same_target = targets[:, :, None] == targets[:, None, :]
    positions = jnp.arange(child_local)
    earlier = positions[None, :] < positions[:, None]
    rank_same = jnp.sum((same_target & earlier[None]).astype(jnp.int32), axis=2)
    offsets = jnp.cumsum(counts, axis=0) - counts
    place_index = jnp.take_along_axis(offsets, targets, axis=1) + rank_same
    slot_orders = jax.vmap(lambda single: jax.random.permutation(single, parent_local))(jax.random.split(key_slot, N_ROW))
    parent_block = targets * parent_local + slot_orders[targets, place_index]
    return parent_block.reshape(-1).astype(jnp.int32)


def draw_block_map(key, part):
    key = jax.random.fold_in(key, 3)
    all_keys = jax.random.split(key, GROUPS * 2)
    drawn = jax.vmap(one_block_map)(all_keys)
    return drawn.reshape(GROUPS, 2, NU // BLK)


def setup_inputs(seed: int = 0) -> dict:
    key_list = jax.random.split(jax.random.key(seed), 4)
    return {
        "front_entries": draw_front_entries(jax.random.fold_in(key_list[3], 71), 0),
        "child_update": draw_child_update(jax.random.fold_in(key_list[3], 71), 0),
        "block_map": draw_block_map(jax.random.fold_in(key_list[3], 71), 0),
    }


def assemble(entries, update_own, update_other, parent_blocks):
    front_count = NF // BLK
    child_count = NU // BLK
    tiled_front = entries.reshape(front_count, BLK, front_count, BLK)
    for child_index, update in ((0, update_own), (1, update_other)):
        pieces = update.reshape(child_count, BLK, child_count, BLK).transpose(0, 2, 1, 3)
        target = parent_blocks[child_index]
        tiled_front = tiled_front.at[target[:, None], :, target[None, :], :].add(pieces)
    return tiled_front.reshape(NF, NF)

def factor_panels(assembled):
    row_ids = jnp.arange(NF)[:, None]
    current = assembled
    for panel_index in range(PANELS):
        start_col = panel_index * PW
        stop_col = start_col + PW
        column = current[:, start_col:stop_col]
        pivot_factor = jnp.linalg.cholesky(column[start_col:stop_col])
        lower_part = jax.scipy.linalg.solve_triangular(pivot_factor, column.T, lower=True).T
        lower_part = jnp.where(row_ids >= start_col, lower_part, 0.0)
        trail_part = jnp.where(row_ids >= stop_col, lower_part, 0.0)
        current = current - jnp.dot(trail_part.astype(jnp.float32), trail_part.T.astype(jnp.float32), precision=lax.Precision.HIGHEST, preferred_element_type=jnp.float32)
        current = current.at[:, start_col:stop_col].set(lower_part)
        current = current.at[start_col:stop_col, stop_col:].set(0.0)
    return current

def reference(front_entries, child_update, block_map):
    results = []
    for group_index in range(GROUPS):
        sibling_index = group_index ^ 1
        assembled = assemble(front_entries[group_index], child_update[group_index], child_update[sibling_index], block_map[group_index])
        results.append(factor_panels(assembled))
    return jnp.stack(results)
```

```python
import functools
import jax
import jax.numpy as jnp
from jax import lax
from jax.experimental import pallas as pl
from jax.experimental.pallas import tpu as pltpu
from jax.sharding import PartitionSpec as P

BLK = 128
CAP = 2
PW = 256
ROWS = 4
CB = 6
PB = 12
OWN = 2
HIGHEST = lax.Precision.HIGHEST
ANY = pl.BlockSpec(memory_space=pl.ANY)
SMEM = pl.BlockSpec(memory_space=pltpu.SMEM)
VMEM = pl.BlockSpec(memory_space=pltpu.VMEM)
F32 = jnp.float32
TICK = jax.ShapeDtypeStruct((8, BLK), F32)


def params(mb=56):
    return pltpu.CompilerParams(vmem_limit_bytes=mb << 20)


def cost(flops, nbytes):
    return pl.CostEstimate(flops=flops, bytes_accessed=nbytes, transcendentals=0)


def ranked(meta, base, sender):
    vals = [meta[base + CB * sender + i] for i in range(CB)]
    targets = [lax.div(v, PB) for v in vals]
    ranks = []
    for i in range(CB):
        rank = jnp.int32(0)
        for j in range(i):
            rank = rank + (targets[j] == targets[i]).astype(jnp.int32)
        ranks.append(rank)
    places = [v - PB * t for v, t in zip(vals, targets)]
    return targets, ranks, places


def place_of(meta, base, q):
    found = jnp.int32(-1)
    for j in range(ROWS * CB):
        found = jnp.where(meta[base + j] == q, jnp.int32(j), found)
    return found


def pack_kernel(base, meta, child, _, out, sems):
    rt, rr, _ = ranked(meta, base, meta[0])
    ct, cr, _ = ranked(meta, base, meta[1])
    copies = []
    for i in range(CB):
        for j in range(CB):
            slot = (rt[i] * ROWS + ct[j]) * 4 + rr[i] * CAP + cr[j]
            copies.append(
                pltpu.make_async_copy(
                    child.at[pl.ds(i * BLK, BLK), pl.ds(j * BLK, BLK)],
                    out.at[slot],
                    sems.at[i * CB + j],
                )
            )
            copies[-1].start()
    for c in copies:
        c.wait()


def pack(meta, child, base, tick):
    return pl.pallas_call(
        functools.partial(pack_kernel, base),
        out_shape=jax.ShapeDtypeStruct((64, BLK, BLK), F32),
        in_specs=[SMEM, VMEM, ANY],
        out_specs=ANY,
        scratch_shapes=[pltpu.SemaphoreType.DMA((CB * CB,))],
        compiler_params=params(),
        cost_estimate=cost(0, 1 << 20),
    )(meta, child, tick)


def strips_kernel(meta, child, sibling, keep, send, sems):
    s = meta[1]
    k = lax.rem(s, 2)
    copies = []
    for hi in range(2):
        for m, source in enumerate((child, sibling)):
            for which, out in ((0, keep), (1, send)):
                q = 2 * hi + lax.rem(k + which, 2)
                j = place_of(meta, OWN + 24 * m, q) - CB * s
                j = jnp.clip(j, 0, CB - 1)
                copies.append(
                    pltpu.make_async_copy(
                        source.at[:, pl.ds(pl.multiple_of(j * BLK, BLK), BLK)],
                        out.at[hi, m],
                        sems.at[hi * 4 + m * 2 + which],
                    )
                )
                copies[-1].start()
    for c in copies:
        c.wait()


def strips(meta, child, sibling):
    shape = jax.ShapeDtypeStruct((2, 2, CB * BLK, BLK), F32)
    return pl.pallas_call(
        strips_kernel,
        out_shape=(shape, shape),
        in_specs=[SMEM, VMEM, VMEM],
        out_specs=(ANY, ANY),
        scratch_shapes=[pltpu.SemaphoreType.DMA((8,))],
        compiler_params=params(),
        cost_estimate=cost(0, 1 << 20),
    )(meta, child, sibling)


def choose_kernel(meta, keep, got, out, sems):
    s = meta[1]
    k = lax.rem(s, 2)
    h = 1 - lax.div(s, 2)
    for m in range(2):
        j = place_of(meta, OWN + 24 * m, 2 * h + k)
        src = lax.rem(lax.div(jnp.maximum(j, 0), CB), 2)

        @pl.when(src == k)
        def _():
            pltpu.make_async_copy(keep.at[h, m], out.at[m], sems.at[m]).start()

        @pl.when(src != k)
        def _():
            pltpu.make_async_copy(got.at[h, m], out.at[m], sems.at[m]).start()

    for m in range(2):
        pltpu.make_async_copy(keep.at[0, m], out.at[m], sems.at[m]).wait()


def choose(meta, keep, got):
    return pl.pallas_call(
        choose_kernel,
        out_shape=jax.ShapeDtypeStruct((2, CB * BLK, BLK), F32),
        in_specs=[SMEM, ANY, ANY],
        out_specs=VMEM,
        scratch_shapes=[pltpu.SemaphoreType.DMA((2,))],
        compiler_params=params(),
        cost_estimate=cost(0, 1 << 20),
    )(meta, keep, got)


def band_kernel(meta, keep, got, far, o0, o1, o2, o3, sems):
    r, s = meta[0], meta[1]
    k = lax.rem(s, 2)
    hi = lax.div(s, 2)
    outs = (o0, o1, o2, o3)
    for m in range(2):
        base = OWN + 24 * m
        j = place_of(meta, base, s)
        src = lax.div(jnp.maximum(j, 0), CB)
        near = lax.div(src, 2) == hi
        same = lax.rem(src, 2) == k
        options = (
            (near & same, keep.at[hi, m]),
            (near & jnp.logical_not(same), got.at[hi, m]),
            (jnp.logical_not(near), far.at[m]),
        )
        targets, ranks, _ = ranked(meta, base, r)
        for i in range(CB):
            shift = lax.rem(targets[i] - r + ROWS, ROWS)
            for take, ref in options:

                @pl.when(take)
                def _():
                    block = ref.at[pl.ds(i * BLK, BLK)]
                    for d in range(ROWS):

                        @pl.when(shift == d)
                        def _():
                            pltpu.make_async_copy(
                                block, outs[d].at[m * CAP + ranks[i]], sems.at[m * CB + i, 0]
                            ).start()

                    @pl.when(targets[i] == 0)
                    def _():
                        for d in range(ROWS):
                            pltpu.make_async_copy(
                                block, outs[d].at[4 + m * CAP + ranks[i]], sems.at[m * CB + i, 1 + d]
                            ).start()

        for i in range(CB):
            done = far.at[0, pl.ds(0, BLK)]
            pltpu.make_async_copy(done, o0.at[0], sems.at[m * CB + i, 0]).wait()

            @pl.when(targets[i] == 0)
            def _():
                for d in range(ROWS):
                    pltpu.make_async_copy(done, o0.at[0], sems.at[m * CB + i, 1 + d]).wait()


def band(meta, keep, got, far):
    shape = jax.ShapeDtypeStruct((4 * CAP, BLK, BLK), F32)
    return pl.pallas_call(
        band_kernel,
        out_shape=(shape,) * 4,
        in_specs=[SMEM] + [ANY] * 3,
        out_specs=(VMEM,) * 4,
        scratch_shapes=[pltpu.SemaphoreType.DMA((2 * CB, 1 + ROWS))],
        compiler_params=params(),
        cost_estimate=cost(0, 1 << 20),
    )(meta, keep, got, far)


def strip_kernel(meta, fs, fd, x0, x1, x2, x3, out):
    r, s = meta[0], meta[1]
    out[: PB * BLK, :] = fs[...]
    out[PB * BLK :, :] = fd[...]
    for m in range(2):
        base = OWN + 24 * m
        there = place_of(meta, base, s) >= 0
        for d, x in enumerate((x0, x1, x2, x3)):
            sender = lax.rem(r - d + ROWS, ROWS)
            targets, ranks, places = ranked(meta, base, sender)
            for i in range(CB):

                @pl.when(there & (targets[i] == r))
                def _():
                    rows = pl.ds(pl.multiple_of(places[i] * BLK, BLK), BLK)
                    out[rows, :] += x[m * CAP + ranks[i]]

                @pl.when(there & (targets[i] == 0) & (places[i] < 4))
                def _():
                    rows = pl.ds(pl.multiple_of((PB + places[i]) * BLK, BLK), BLK)
                    out[rows, :] += x[4 + m * CAP + ranks[i]]


def strip_add(meta, fs, fd, xs):
    return pl.pallas_call(
        strip_kernel,
        out_shape=jax.ShapeDtypeStruct(((PB + 4) * BLK, BLK), F32),
        in_specs=[SMEM] + [VMEM] * 6,
        out_specs=VMEM,
        compiler_params=params(),
        cost_estimate=cost(0, 1 << 20),
    )(meta, fs, fd, *xs)


def dot(a, b, dims=((1,), (0,))):
    return lax.dot_general(a, b, (dims, ((), ())), precision=HIGHEST, preferred_element_type=F32)


def dot_t(a, b):
    return dot(a, b, ((1,), (1,)))


def inverse_factor(block):
    groups = BLK // 8
    left = [block[8 * g : 8 * g + 8, :] for g in range(groups)]
    sub = lax.broadcasted_iota(jnp.int32, (8, BLK), 0)
    lane = lax.broadcasted_iota(jnp.int32, (8, BLK), 1)
    right = [(lane == sub + 8 * g).astype(F32) for g in range(groups)]
    for k in range(BLK):
        g0, kk = divmod(k, 8)
        row_l = left[g0][kk : kk + 1, :]
        row_r = right[g0][kk : kk + 1, :]
        inv = 1.0 / row_l[:, k : k + 1]
        row_l = row_l * inv
        row_r = row_r * inv
        for g in range(g0, groups):
            if g == g0 and kk == 7:
                continue
            col = left[g][:, k : k + 1]
            if g == g0:
                col = jnp.where(sub[:, :1] > kk, col, 0.0)
            left[g] = left[g] - col * row_l
            right[g] = right[g] - col * row_r
    out = []
    for g in range(groups):
        diag = jnp.sum(jnp.where(lane == sub + 8 * g, left[g], 0.0), axis=1, keepdims=True)
        out.append(right[g] / jnp.sqrt(diag))
    return jnp.concatenate(out, axis=0)


def pick(s, own, got, q, rows=slice(None)):
    far = jnp.not_equal(lax.div(s, 2), q // 2).astype(jnp.int32)
    return jnp.where(lax.rem(s, 2) == q % 2, own[far, rows], got[far, rows])


def inverse_panel(a, low, w, out):
    def step(b, carry):
        at = pl.ds(pl.multiple_of(b * BLK, BLK), BLK)
        w[b] = inverse_factor(a[at, at])

        @pl.when(b == 0)
        def _():
            below = dot_t(a[BLK:, :BLK], w[0])
            low[...] = below
            a[BLK:, BLK:] -= dot_t(below, below)

        return carry

    lax.fori_loop(0, 2, step, 0)
    out[:BLK, :BLK] = w[0]
    out[:BLK, BLK:] = jnp.zeros((BLK, BLK), F32)
    out[BLK:, :BLK] = -dot(dot(w[1], low[...]), w[0])
    out[BLK:, BLK:] = w[1]


def symmetric(d):
    return 0.5 * (d + d.T)


def first_kernel(meta, own, got, w0, l10, rest, tick, a, low, w):
    s = meta[1]
    d = jnp.concatenate([pick(s, own, got, q) for q in range(4)], axis=1)
    a[...] = symmetric(d[:PW, :PW])
    inverse_panel(a, low, w, w0)
    below = dot_t(d[PW:, :PW], w0[...])
    l10[...] = below
    rest[...] = symmetric(d[PW:, PW:] - dot_t(below, below))
    tick[...] = jnp.zeros_like(tick)


def second_kernel(rest, _, w1, tick, a, low, w):
    a[...] = rest[...]
    inverse_panel(a, low, w, w1)
    tick[...] = jnp.zeros_like(tick)


FACTOR_SCRATCH = [
    pltpu.VMEM((PW, PW), F32),
    pltpu.VMEM((BLK, BLK), F32),
    pltpu.VMEM((2, BLK, BLK), F32),
]


def factor_first(meta, own, got):
    shape = jax.ShapeDtypeStruct((PW, PW), F32)
    diag = pl.BlockSpec((2, 2 * PW, BLK), lambda i: (0, 3, 0))
    whole = pl.BlockSpec((PW, PW), lambda i: (0, 0))
    return pl.pallas_call(
        first_kernel,
        grid=(1,),
        out_shape=(shape, shape, shape, TICK),
        in_specs=[SMEM, diag, diag],
        out_specs=(whole, whole, whole, pl.BlockSpec((8, BLK), lambda i: (0, 0))),
        scratch_shapes=FACTOR_SCRATCH,
        compiler_params=params(),
        cost_estimate=cost(0, 90 << 20),
    )(meta, own, got)


def factor_second(rest, tick):
    return pl.pallas_call(
        second_kernel,
        out_shape=(jax.ShapeDtypeStruct((PW, PW), F32), TICK),
        in_specs=[VMEM, VMEM],
        out_specs=(VMEM, VMEM),
        scratch_shapes=FACTOR_SCRATCH,
        compiler_params=params(),
        cost_estimate=cost(0, 90 << 20),
    )(rest, tick)


def split(x):
    high = x.astype(jnp.bfloat16)
    return high, (x - high.astype(F32)).astype(jnp.bfloat16)


def solve(x, w0, l10, w1):
    first = dot_t(x[:, :PW], w0)
    second = dot_t(x[:, PW:] - dot_t(first, l10), w1)
    return first, second


def rows_kernel(meta, own, got, w0, l10, w1, _, low, high, rest):
    i = pl.program_id(0)
    x = jnp.concatenate([pick(meta[1], own, got, q) for q in range(4)], axis=1)
    first, second = solve(x, w0[...], l10[...], w1[...])
    second = jnp.where((i == 0) & (meta[0] == 0), 0.0, second)
    whole = jnp.concatenate([first, second], axis=1)
    low[...] = whole
    high[...], rest[...] = split(whole)


def factor_rows(meta, own, got, w0, l10, w1, tick):
    n = PB * BLK
    src = pl.BlockSpec((2, PW, BLK), lambda i: (0, i, 0))
    whole = pl.BlockSpec((PW, PW), lambda i: (0, 0))
    out = pl.BlockSpec((PW, 2 * PW), lambda i: (i, 0))
    return pl.pallas_call(
        rows_kernel,
        grid=(n // PW,),
        out_shape=(
            jax.ShapeDtypeStruct((n, 2 * PW), F32),
            jax.ShapeDtypeStruct((n, 2 * PW), jnp.bfloat16),
            jax.ShapeDtypeStruct((n, 2 * PW), jnp.bfloat16),
        ),
        in_specs=[SMEM, src, src, whole, whole, whole, pl.BlockSpec((8, BLK), lambda i: (0, 0))],
        out_specs=(out, out, out),
        compiler_params=params(),
        cost_estimate=cost(0, 1 << 20),
    )(meta, own, got, w0, l10, w1, tick)


def cols_kernel(meta, o0, g0, o1, g1, o2, g2, o3, g3, w0, l10, w1, high, rest):
    r, s = meta[0], meta[1]
    away = lax.rem(r - s + ROWS, ROWS)
    owns, gots = (o0, o1, o2, o3), (g0, g1, g2, g3)
    own, got = o0[...], g0[...]
    for d in range(1, ROWS):
        own = jnp.where(away == d, owns[d][...], own)
        got = jnp.where(away == d, gots[d][...], got)
    k = lax.rem(s, 2) == 0
    hi = lax.div(s, 2) == 0
    parts = []
    for q in range(4):
        mine, other = (own, got) if q % 2 == 0 else (got, own)
        both = jnp.where(k, mine, other)
        parts.append(jnp.where(hi, both[q // 2], both[1 - q // 2]))
    x = jnp.concatenate(parts, axis=1)
    first, second = solve(x, w0[...], l10[...], w1[...])
    whole = jnp.concatenate([first, second], axis=1).T
    high[...], rest[...] = split(whole)


def factor_cols(meta, pairs, w0, l10, w1):
    n = PB * BLK

    def src(d):
        return pl.BlockSpec(
            (2, PW, BLK),
            lambda i, meta: (0, jnp.where(lax.rem(meta[0] - meta[1] + ROWS, ROWS) == d, i, 0), 0),
        )

    whole = pl.BlockSpec((PW, PW), lambda i, meta: (0, 0))
    out = pl.BlockSpec((2 * PW, PW), lambda i, meta: (0, i))
    return pl.pallas_call(
        cols_kernel,
        grid_spec=pltpu.PrefetchScalarGridSpec(
            num_scalar_prefetch=1,
            grid=(n // PW,),
            in_specs=[src(d) for d in range(ROWS) for _ in range(2)] + [whole] * 3,
            out_specs=(out, out),
        ),
        out_shape=(jax.ShapeDtypeStruct((2 * PW, n), jnp.bfloat16),) * 2,
        compiler_params=params(),
        cost_estimate=cost(0, 1 << 20),
    )(meta, *[x for pair in pairs for x in pair], w0, l10, w1)


def table_kernel(meta, out):
    for n in range(6 * PB + 16):
        out[n] = jnp.int32(-1)
    for c in range(2):
        base = OWN + 24 * c
        for axis in range(2):
            here = meta[axis]
            for sender in range(ROWS):
                targets, ranks, places = ranked(meta, base, sender)
                for i in range(CB):

                    @pl.when(targets[i] == here)
                    def _():
                        out[(3 * c + axis) * PB + places[i]] = CAP * sender + ranks[i]
                        if c == 1 and axis == 0:
                            out[6 * PB + CAP * sender + ranks[i]] = places[i]

        last = jnp.int32(0)
        for p in range(PB):
            slot = out[3 * c * PB + p]
            last = jnp.where(slot >= 0, slot, last)
            out[(3 * c + 2) * PB + p] = last
    first = jnp.int32(0)
    for j in reversed(range(8)):
        first = jnp.where(out[6 * PB + j] >= 0, out[6 * PB + j], first)
    for j in range(8):
        at = out[6 * PB + j]
        out[6 * PB + 8 + j] = (at >= 0).astype(jnp.int32)
        first = jnp.where(at >= 0, at, first)
        out[6 * PB + j] = first


def tables(meta):
    return pl.pallas_call(
        table_kernel,
        out_shape=jax.ShapeDtypeStruct((6 * PB + 16,), jnp.int32),
        in_specs=[SMEM],
        out_specs=SMEM,
    )(meta)


def trail_kernel(meta, tab, front, xa, low, rh, rl, ch, cl, out):
    p = pl.program_id(0)
    r, s = meta[0], meta[1]
    top = (r == 0) & (p < 4)

    @pl.when(top)
    def _():
        out[...] = jnp.zeros_like(out)

    @pl.when(jnp.logical_not(top))
    def _():
        def mul(a, b):
            return lax.dot_general(a, b, (((1,), (0,)), ((), ())), preferred_element_type=F32)

        for c in range(PB * BLK // PW):
            at = slice(c * PW, (c + 1) * PW)
            prod = mul(rh[...], ch[:, at]) + (mul(rh[...], cl[:, at]) + mul(rl[...], ch[:, at]))
            out[:, at] = front[:, at] - prod
        there = tab[p] >= 0
        for q in range(PB):
            slot = tab[PB + q]

            @pl.when(there & (slot >= 0))
            def _():
                at = slice(q * BLK, (q + 1) * BLK)
                out[:, at] += xa[0, lax.div(slot, 2), 0, lax.rem(slot, 2)]

    @pl.when(s == 0)
    def _():
        out[:, : 2 * PW] = low[...]


def trail(meta, tab, front, xa, low, rh, rl, ch, cl):
    n = PB * BLK

    def index(p, meta, tab):
        slot = tab[2 * PB + p]
        return (lax.div(slot, 2), 0, lax.rem(slot, 2), 0, 0, 0)

    wide = pl.BlockSpec((BLK, n), lambda p, meta, tab: (p, 0))
    rows = pl.BlockSpec((BLK, 2 * PW), lambda p, meta, tab: (p, 0))
    cols = pl.BlockSpec((2 * PW, n), lambda p, meta, tab: (0, 0))
    return pl.pallas_call(
        trail_kernel,
        grid_spec=pltpu.PrefetchScalarGridSpec(
            num_scalar_prefetch=2,
            grid=(PB,),
            in_specs=[wide, pl.BlockSpec((1, 4, 1, 2, BLK, BLK), index)]
            + [rows, rows, rows, cols, cols],
            out_specs=wide,
        ),
        out_shape=jax.ShapeDtypeStruct((n, n), F32),
        compiler_params=params(),
        cost_estimate=cost(0, 1 << 20),
    )(meta, tab, front, xa, low, rh, rl, ch, cl)


def last_kernel(meta, tab, front, xb, out):
    j = pl.program_id(0)
    p = tab[6 * PB + j]
    fresh = (j == 0) | (p != tab[6 * PB + jnp.maximum(j - 1, 0)])

    @pl.when(fresh)
    def _():
        out[...] = front[...]

    add = (tab[6 * PB + 8 + j] > 0) & jnp.logical_not((meta[0] == 0) & (p < 4))
    for q in range(PB):
        slot = tab[4 * PB + q]

        @pl.when(add & (slot >= 0) & ((meta[1] > 0) | (q >= 4)))
        def _():
            at = slice(q * BLK, (q + 1) * BLK)
            out[:, at] += xb[0, lax.div(slot, 2), 0, lax.rem(slot, 2)]


def last(meta, tab, front, xb):
    n = PB * BLK
    wide = pl.BlockSpec((BLK, n), lambda j, meta, tab: (tab[6 * PB + j], 0))
    return pl.pallas_call(
        last_kernel,
        grid_spec=pltpu.PrefetchScalarGridSpec(
            num_scalar_prefetch=2,
            grid=(2 * ROWS,),
            in_specs=[
                wide,
                pl.BlockSpec(
                    (1, 4, 1, 2, BLK, BLK),
                    lambda j, meta, tab: (lax.div(j, 2), 0, lax.rem(j, 2), 0, 0, 0),
                ),
            ],
            out_specs=wide,
        ),
        out_shape=jax.ShapeDtypeStruct((n, n), F32),
        input_output_aliases={2: 0},
        compiler_params=params(),
        cost_estimate=cost(0, 1 << 20),
    )(meta, tab, front, xb)


def move(x, axes, fn, sizes, only=None):
    pairs = []
    total = 1
    for size in sizes:
        total *= size

    def unflat(i):
        place = []
        for size in reversed(sizes):
            place.append(i % size)
            i //= size
        return tuple(reversed(place))

    def flat(place):
        i = 0
        for at, size in zip(place, sizes):
            i = i * size + at
        return i

    for i in range(total):
        place = unflat(i)
        if only is None or only(*place):
            pairs.append((i, flat(fn(*place))))
    return lax.ppermute(x, axes if len(axes) > 1 else axes[0], pairs)


def across_cube(x):
    return move(x, ("cube",), lambda g: (g ^ 1,), (8,))


def across_col(x, mask):
    return move(x, ("col",), lambda s: (s ^ mask,), (4,))


def exchange(packed):
    per = packed.shape[0] // 16
    got = lax.all_to_all(packed.reshape(16, per, BLK, BLK), ("row", "col"), 0, 0, tiled=True)
    return got.reshape(4, 4, per // 2, 2, BLK, BLK)


def shards(front_entries, child_update, block_map):
    barrier = lax.optimization_barrier
    front = front_entries[0]
    child = child_update[0]
    row_here, col_here = lax.axis_index("row"), lax.axis_index("col")
    here = jnp.stack([row_here, col_here]).astype(jnp.int32)
    meta = jnp.concatenate([here, block_map.reshape(-1)])
    n = PB * BLK

    sibling = across_cube(child)

    fs = [front[:, q * BLK : (q + 1) * BLK] for q in range(4)]
    moved = [move(fs[q], ("col",), lambda s: (q,), (4,), lambda s: s == 0) for q in range(1, 4)]
    xa = exchange(pack(meta, child, OWN, meta))

    keep, send = strips(meta, child, sibling)
    got = across_col(send, 1)
    chosen = choose(meta, keep, got)
    far = across_col(chosen, 2)
    xa, far = barrier((xa, far))
    outs = band(meta, keep, got, far)
    moved, outs = barrier((moved, outs))
    fs = jnp.where(col_here == 0, fs[0], moved[0] + moved[1] + moved[2])
    top = fs[: 2 * PW]
    tops = [move(top, ("row",), lambda r: (d,), (4,), lambda r: r == 0) for d in range(1, 4)]
    fd = jnp.where(row_here == 0, top, tops[0] + tops[1] + tops[2])
    xs = [outs[0]] + [
        move(outs[d], ("row",), lambda r: ((r + d) % 4,), (4,)) for d in range(1, 4)
    ]
    mine = strip_add(meta, fs, fd, xs)

    own = jnp.stack([mine, across_col(mine, 2)])
    other = across_col(own, 1)
    tab = tables(meta)

    def step(x, start, stop):
        return move(
            x,
            ("row", "col"),
            lambda r, s: ((s + stop) % 4, s),
            (4, 4),
            lambda r, s: r == (s + start) % 4,
        )

    own_band, other_band = own[:, :n], other[:, :n]
    o1, o3 = step(own_band, 0, 1), step(own_band, 0, 3)
    g1, g3 = step(other_band, 0, 1), step(other_band, 0, 3)
    w0, l10, rest, tick = factor_first(meta, own, other)
    tick = across_col(tick, 1)
    o1, o3, g1, g3, rest, tick = barrier((o1, o3, g1, g3, rest, tick))
    o2, g2 = step(o1, 1, 2), step(g3, 3, 2)
    w1, tick = factor_second(rest, tick)
    tick = across_col(tick, 1)
    w0, l10, w1, tick, o2, g2, sibling = barrier((w0, l10, w1, tick, o2, g2, sibling))
    packed = pack(meta, sibling, OWN + 24, tick)
    packed, w1 = barrier((packed, w1))
    xb = exchange(packed)
    low, rh, rl = factor_rows(meta, own, other, w0, l10, w1, tick)
    ch, cl = factor_cols(
        meta, ((own, other), (o1, g1), (o2, g2), (o3, g3)), w0, l10, w1
    )
    whole = trail(meta, tab, front, xa, low, rh, rl, ch, cl)
    return last(meta, tab, whole, xb)[None]


def solution(mesh):
    in_specs = (P("cube", "row", "col"), P("cube", "row", "col"), P("cube", None, None))
    out_specs = P("cube", "row", "col")
    return jax.shard_map(shards, mesh=mesh, in_specs=in_specs, out_specs=out_specs, check_vma=False)
```

```python
import functools
import jax
import jax.numpy as jnp
from jax import lax
from jax.experimental import pallas as pl
from jax.experimental.pallas import tpu as pltpu
from jax.sharding import PartitionSpec as P

BLK = 128
CAP = 2
PW = 256
ROWS = 4
CB = 6
PB = 12
OWN = 2
HIGHEST = lax.Precision.HIGHEST
ANY = pl.BlockSpec(memory_space=pl.ANY)
SMEM = pl.BlockSpec(memory_space=pltpu.SMEM)
VMEM = pl.BlockSpec(memory_space=pltpu.VMEM)
F32 = jnp.float32
TICK = jax.ShapeDtypeStruct((8, BLK), F32)


def params(mb=56):
    return pltpu.CompilerParams(vmem_limit_bytes=mb << 20)


def cost(flops, nbytes):
    return pl.CostEstimate(flops=flops, bytes_accessed=nbytes, transcendentals=0)


def ranked(meta, base, sender):
    vals = [meta[base + CB * sender + i] for i in range(CB)]
    targets = [lax.div(v, PB) for v in vals]
    ranks = []
    for i in range(CB):
        rank = jnp.int32(0)
        for j in range(i):
            rank = rank + (targets[j] == targets[i]).astype(jnp.int32)
        ranks.append(rank)
    places = [v - PB * t for v, t in zip(vals, targets)]
    return targets, ranks, places


def place_of(meta, base, q):
    found = jnp.int32(-1)
    for j in range(ROWS * CB):
        found = jnp.where(meta[base + j] == q, jnp.int32(j), found)
    return found


def pack_kernel(base, meta, child, _, out, sems):
    rt, rr, _ = ranked(meta, base, meta[0])
    ct, cr, _ = ranked(meta, base, meta[1])
    copies = []
    for i in range(CB):
        for j in range(CB):
            slot = (rt[i] * ROWS + ct[j]) * 4 + rr[i] * CAP + cr[j]
            copies.append(
                pltpu.make_async_copy(
                    child.at[pl.ds(i * BLK, BLK), pl.ds(j * BLK, BLK)],
                    out.at[slot],
                    sems.at[i * CB + j],
                )
            )
            copies[-1].start()
    for c in copies:
        c.wait()


def pack(meta, child, base, tick):
    return pl.pallas_call(
        functools.partial(pack_kernel, base),
        out_shape=jax.ShapeDtypeStruct((64, BLK, BLK), F32),
        in_specs=[SMEM, VMEM, ANY],
        out_specs=ANY,
        scratch_shapes=[pltpu.SemaphoreType.DMA((CB * CB,))],
        compiler_params=params(),
        cost_estimate=cost(0, 1 << 20),
    )(meta, child, tick)


def row_pack_kernel(base, meta, child, o0, o1, o2, o3, sems):
    outs = (o0, o1, o2, o3)
    r = meta[0]
    targets, ranks, _ = ranked(meta, base, r)
    for i in range(CB):
        shift = lax.rem(targets[i] - r + ROWS, ROWS)
        for d in range(ROWS):

            @pl.when(shift == d)
            def _():
                pltpu.make_async_copy(
                    child.at[pl.ds(i * BLK, BLK)], outs[d].at[ranks[i]], sems.at[i]
                ).start()

    for i in range(CB):
        pltpu.make_async_copy(child.at[pl.ds(0, BLK)], o0.at[0], sems.at[i]).wait()


def row_pack(meta, child, base):
    shape = jax.ShapeDtypeStruct((CAP, BLK, CB * BLK), F32)
    return pl.pallas_call(
        functools.partial(row_pack_kernel, base),
        out_shape=(shape,) * 4,
        in_specs=[SMEM, VMEM],
        out_specs=(ANY,) * 4,
        scratch_shapes=[pltpu.SemaphoreType.DMA((CB,))],
        compiler_params=params(),
        cost_estimate=cost(0, 1 << 20),
    )(meta, child)


def col_pack_kernel(base, meta, x0, x1, x2, x3, o0, o1, o2, o3, sems):
    outs = (o0, o1, o2, o3)
    s = meta[1]
    targets, ranks, _ = ranked(meta, base, s)
    for j in range(CB):
        mask = jnp.bitwise_xor(targets[j], s)
        for m in range(ROWS):

            @pl.when(mask == m)
            def _():
                for d, x in enumerate((x0, x1, x2, x3)):
                    for k in range(CAP):
                        pltpu.make_async_copy(
                            x.at[k, :, pl.ds(j * BLK, BLK)],
                            outs[m].at[d * CAP + k, ranks[j]],
                            sems.at[j, d * CAP + k],
                        ).start()

    for j in range(CB):
        for n in range(2 * ROWS):
            pltpu.make_async_copy(x0.at[0, :, pl.ds(0, BLK)], o0.at[0, 0], sems.at[j, n]).wait()


def col_pack(meta, xs, base):
    shape = jax.ShapeDtypeStruct((2 * ROWS, CAP, BLK, BLK), F32)
    return pl.pallas_call(
        functools.partial(col_pack_kernel, base),
        out_shape=(shape,) * 4,
        in_specs=[SMEM] + [VMEM] * 4,
        out_specs=(ANY,) * 4,
        scratch_shapes=[pltpu.SemaphoreType.DMA((CB, 2 * ROWS))],
        compiler_params=params(),
        cost_estimate=cost(0, 1 << 20),
    )(meta, *xs)


def strips_kernel(meta, child, sibling, keep, send, sems):
    s = meta[1]
    k = lax.rem(s, 2)
    copies = []
    for hi in range(2):
        for m, source in enumerate((child, sibling)):
            for which, out in ((0, keep), (1, send)):
                q = 2 * hi + lax.rem(k + which, 2)
                j = place_of(meta, OWN + 24 * m, q) - CB * s
                j = jnp.clip(j, 0, CB - 1)
                copies.append(
                    pltpu.make_async_copy(
                        source.at[:, pl.ds(pl.multiple_of(j * BLK, BLK), BLK)],
                        out.at[hi, m],
                        sems.at[hi * 4 + m * 2 + which],
                    )
                )
                copies[-1].start()
    for c in copies:
        c.wait()


def strips(meta, child, sibling):
    shape = jax.ShapeDtypeStruct((2, 2, CB * BLK, BLK), F32)
    return pl.pallas_call(
        strips_kernel,
        out_shape=(shape, shape),
        in_specs=[SMEM, VMEM, VMEM],
        out_specs=(ANY, ANY),
        scratch_shapes=[pltpu.SemaphoreType.DMA((8,))],
        compiler_params=params(),
        cost_estimate=cost(0, 1 << 20),
    )(meta, child, sibling)


def choose_kernel(meta, keep, got, out, sems):
    s = meta[1]
    k = lax.rem(s, 2)
    h = 1 - lax.div(s, 2)
    for m in range(2):
        j = place_of(meta, OWN + 24 * m, 2 * h + k)
        src = lax.rem(lax.div(jnp.maximum(j, 0), CB), 2)

        @pl.when(src == k)
        def _():
            pltpu.make_async_copy(keep.at[h, m], out.at[m], sems.at[m]).start()

        @pl.when(src != k)
        def _():
            pltpu.make_async_copy(got.at[h, m], out.at[m], sems.at[m]).start()

    for m in range(2):
        pltpu.make_async_copy(keep.at[0, m], out.at[m], sems.at[m]).wait()


def choose(meta, keep, got):
    return pl.pallas_call(
        choose_kernel,
        out_shape=jax.ShapeDtypeStruct((2, CB * BLK, BLK), F32),
        in_specs=[SMEM, ANY, ANY],
        out_specs=VMEM,
        scratch_shapes=[pltpu.SemaphoreType.DMA((2,))],
        compiler_params=params(),
        cost_estimate=cost(0, 1 << 20),
    )(meta, keep, got)


def band_kernel(meta, keep, got, far, o0, o1, o2, o3, sems):
    r, s = meta[0], meta[1]
    k = lax.rem(s, 2)
    hi = lax.div(s, 2)
    outs = (o0, o1, o2, o3)
    for m in range(2):
        base = OWN + 24 * m
        j = place_of(meta, base, s)
        src = lax.div(jnp.maximum(j, 0), CB)
        near = lax.div(src, 2) == hi
        same = lax.rem(src, 2) == k
        options = (
            (near & same, keep.at[hi, m]),
            (near & jnp.logical_not(same), got.at[hi, m]),
            (jnp.logical_not(near), far.at[m]),
        )
        targets, ranks, _ = ranked(meta, base, r)
        for i in range(CB):
            shift = lax.rem(targets[i] - r + ROWS, ROWS)
            for take, ref in options:

                @pl.when(take)
                def _():
                    block = ref.at[pl.ds(i * BLK, BLK)]
                    for d in range(ROWS):

                        @pl.when(shift == d)
                        def _():
                            pltpu.make_async_copy(
                                block, outs[d].at[m * CAP + ranks[i]], sems.at[m * CB + i, 0]
                            ).start()

                    @pl.when(targets[i] == 0)
                    def _():
                        for d in range(ROWS):
                            pltpu.make_async_copy(
                                block, outs[d].at[4 + m * CAP + ranks[i]], sems.at[m * CB + i, 1 + d]
                            ).start()

        for i in range(CB):
            done = far.at[0, pl.ds(0, BLK)]
            pltpu.make_async_copy(done, o0.at[0], sems.at[m * CB + i, 0]).wait()

            @pl.when(targets[i] == 0)
            def _():
                for d in range(ROWS):
                    pltpu.make_async_copy(done, o0.at[0], sems.at[m * CB + i, 1 + d]).wait()


def band(meta, keep, got, far):
    shape = jax.ShapeDtypeStruct((4 * CAP, BLK, BLK), F32)
    return pl.pallas_call(
        band_kernel,
        out_shape=(shape,) * 4,
        in_specs=[SMEM] + [ANY] * 3,
        out_specs=(VMEM,) * 4,
        scratch_shapes=[pltpu.SemaphoreType.DMA((2 * CB, 1 + ROWS))],
        compiler_params=params(),
        cost_estimate=cost(0, 1 << 20),
    )(meta, keep, got, far)


def strip_kernel(meta, f0, f1, f2, f3, x0, x1, x2, x3, out, sem):
    r, s = meta[0], meta[1]
    for n, f in enumerate((f0, f1, f2, f3)):

        @pl.when(s == n)
        def _():
            pltpu.make_async_copy(f, out, sem).start()

    pltpu.make_async_copy(f0, out, sem).wait()
    for m in range(2):
        base = OWN + 24 * m
        there = place_of(meta, base, s) >= 0
        for d, x in enumerate((x0, x1, x2, x3)):
            sender = lax.rem(r - d + ROWS, ROWS)
            targets, ranks, places = ranked(meta, base, sender)
            for i in range(CB):

                @pl.when(there & (targets[i] == r))
                def _():
                    rows = pl.ds(pl.multiple_of(places[i] * BLK, BLK), BLK)
                    out[rows, :] += x[m * CAP + ranks[i]]

                @pl.when(there & (targets[i] == 0) & (places[i] < 4))
                def _():
                    rows = pl.ds(pl.multiple_of((PB + places[i]) * BLK, BLK), BLK)
                    out[rows, :] += x[4 + m * CAP + ranks[i]]


def strip_add(meta, fs, xs):
    return pl.pallas_call(
        strip_kernel,
        out_shape=jax.ShapeDtypeStruct(((PB + 4) * BLK, BLK), F32),
        in_specs=[SMEM] + [ANY] * 4 + [VMEM] * 4,
        out_specs=VMEM,
        scratch_shapes=[pltpu.SemaphoreType.DMA(())],
        compiler_params=params(),
        cost_estimate=cost(0, 1 << 20),
    )(meta, *fs, *xs)


def dot(a, b, dims=((1,), (0,))):
    return lax.dot_general(a, b, (dims, ((), ())), precision=HIGHEST, preferred_element_type=F32)


def dot_t(a, b):
    return dot(a, b, ((1,), (1,)))


def inverse_factor(block):
    groups = BLK // 8
    left = [block[8 * g : 8 * g + 8, :] for g in range(groups)]
    sub = lax.broadcasted_iota(jnp.int32, (8, BLK), 0)
    lane = lax.broadcasted_iota(jnp.int32, (8, BLK), 1)
    right = [(lane == sub + 8 * g).astype(F32) for g in range(groups)]
    for at in range(groups):
        cols = [
            {g: jnp.broadcast_to(left[g][:, k : k + 1], (8, BLK)) for g in range(at, groups)}
            for k in range(8 * at, 8 * at + 8)
        ]
        row_l = [left[at][j : j + 1, :] for j in range(8)]
        row_r = [right[at][j : j + 1, :] for j in range(8)]
        for j in range(8):
            inv = 1.0 / cols[j][at][j : j + 1, :]
            row_l[j] = row_l[j] * inv
            row_r[j] = row_r[j] * inv
            for m in range(j + 1, 8):
                entry = cols[j][at][m : m + 1, :]
                row_l[m] = row_l[m] - entry * row_l[j]
                row_r[m] = row_r[m] - entry * row_r[j]
                scaled = entry * inv
                for g in range(at, groups):
                    cols[m][g] = cols[m][g] - cols[j][g] * scaled
        for g in range(at, groups):
            for j in range(8):
                col = cols[j][g] if g > at else jnp.where(sub > j, cols[j][g], 0.0)
                left[g] = left[g] - col * row_l[j]
                right[g] = right[g] - col * row_r[j]
    out = []
    for g in range(groups):
        diag = jnp.sum(jnp.where(lane == sub + 8 * g, left[g], 0.0), axis=1, keepdims=True)
        out.append(right[g] / jnp.sqrt(diag))
    return jnp.concatenate(out, axis=0)


def pick(s, own, got, q, rows=slice(None)):
    far = jnp.not_equal(lax.div(s, 2), q // 2).astype(jnp.int32)
    return jnp.where(lax.rem(s, 2) == q % 2, own[far, rows], got[far, rows])


def inverse_panel(a, low, w, out):
    def step(b, carry):
        at = pl.ds(pl.multiple_of(b * BLK, BLK), BLK)
        w[b] = inverse_factor(a[at, at])

        @pl.when(b == 0)
        def _():
            below = dot_t(a[BLK:, :BLK], w[0])
            low[...] = below
            a[BLK:, BLK:] -= dot_t(below, below)

        return carry

    lax.fori_loop(0, 2, step, 0)
    out[:BLK, :BLK] = w[0]
    out[:BLK, BLK:] = jnp.zeros((BLK, BLK), F32)
    out[BLK:, :BLK] = -dot(dot(w[1], low[...]), w[0])
    out[BLK:, BLK:] = w[1]


def symmetric(d):
    return 0.5 * (d + d.T)


def factor_kernel(meta, own, got, w0, l10, w1, tick, a, low, w):
    s = meta[1]
    d = jnp.concatenate([pick(s, own, got, q) for q in range(4)], axis=1)
    a[...] = symmetric(d[:PW, :PW])
    inverse_panel(a, low, w, w0)
    below = dot_t(d[PW:, :PW], w0[...])
    l10[...] = below
    a[...] = symmetric(d[PW:, PW:] - dot_t(below, below))
    inverse_panel(a, low, w, w1)
    tick[...] = jnp.zeros_like(tick)


def factor(meta, own, got):
    shape = jax.ShapeDtypeStruct((PW, PW), F32)
    diag = pl.BlockSpec((2, 2 * PW, BLK), lambda i: (0, 3, 0))
    whole = pl.BlockSpec((PW, PW), lambda i: (0, 0))
    return pl.pallas_call(
        factor_kernel,
        grid=(1,),
        out_shape=(shape, shape, shape, TICK),
        in_specs=[SMEM, diag, diag],
        out_specs=(whole, whole, whole, pl.BlockSpec((8, BLK), lambda i: (0, 0))),
        scratch_shapes=[
            pltpu.VMEM((PW, PW), F32),
            pltpu.VMEM((BLK, BLK), F32),
            pltpu.VMEM((2, BLK, BLK), F32),
        ],
        compiler_params=params(),
        cost_estimate=cost(0, 90 << 20),
    )(meta, own, got)


def split(x):
    high = x.astype(jnp.bfloat16)
    return high, (x - high.astype(F32)).astype(jnp.bfloat16)


def solve(x, w0, l10, w1):
    first = dot_t(x[:, :PW], w0)
    second = dot_t(x[:, PW:] - dot_t(first, l10), w1)
    return first, second


def rows_kernel(meta, own, got, w0, l10, w1, _, low, high, rest, tick):
    tick[...] = jnp.zeros_like(tick)
    i = pl.program_id(0)
    x = jnp.concatenate([pick(meta[1], own, got, q) for q in range(4)], axis=1)
    first, second = solve(x, w0[...], l10[...], w1[...])
    second = jnp.where((i == 0) & (meta[0] == 0), 0.0, second)
    whole = jnp.concatenate([first, second], axis=1)
    low[...] = whole
    high[...], rest[...] = split(whole)


def factor_rows(meta, own, got, w0, l10, w1, tick):
    n = PB * BLK
    src = pl.BlockSpec((2, PW, BLK), lambda i: (0, i, 0))
    whole = pl.BlockSpec((PW, PW), lambda i: (0, 0))
    out = pl.BlockSpec((PW, 2 * PW), lambda i: (i, 0))
    return pl.pallas_call(
        rows_kernel,
        grid=(n // PW,),
        out_shape=(
            jax.ShapeDtypeStruct((n, 2 * PW), F32),
            jax.ShapeDtypeStruct((n, 2 * PW), jnp.bfloat16),
            jax.ShapeDtypeStruct((n, 2 * PW), jnp.bfloat16),
            TICK,
        ),
        in_specs=[SMEM, src, src, whole, whole, whole, pl.BlockSpec((8, BLK), lambda i: (0, 0))],
        out_specs=(out, out, out, pl.BlockSpec((8, BLK), lambda i: (0, 0))),
        compiler_params=params(),
        cost_estimate=cost(0, 1 << 20),
    )(meta, own, got, w0, l10, w1, tick)


def cols_kernel(meta, o0, g0, o1, g1, o2, g2, o3, g3, w0, l10, w1, _, high, rest):
    r, s = meta[0], meta[1]
    away = lax.rem(r - s + ROWS, ROWS)
    owns, gots = (o0, o1, o2, o3), (g0, g1, g2, g3)
    own, got = o0[...], g0[...]
    for d in range(1, ROWS):
        own = jnp.where(away == d, owns[d][...], own)
        got = jnp.where(away == d, gots[d][...], got)
    k = lax.rem(s, 2) == 0
    hi = lax.div(s, 2) == 0
    parts = []
    for q in range(4):
        mine, other = (own, got) if q % 2 == 0 else (got, own)
        both = jnp.where(k, mine, other)
        parts.append(jnp.where(hi, both[q // 2], both[1 - q // 2]))
    x = jnp.concatenate(parts, axis=1)
    first, second = solve(x, w0[...], l10[...], w1[...])
    whole = jnp.concatenate([first, second], axis=1).T
    high[...], rest[...] = split(whole)


def factor_cols(meta, pairs, w0, l10, w1, tick):
    n = PB * BLK

    def src(d):
        return pl.BlockSpec(
            (2, PW, BLK),
            lambda i, meta: (0, jnp.where(lax.rem(meta[0] - meta[1] + ROWS, ROWS) == d, i, 0), 0),
        )

    whole = pl.BlockSpec((PW, PW), lambda i, meta: (0, 0))
    out = pl.BlockSpec((2 * PW, PW), lambda i, meta: (0, i))
    return pl.pallas_call(
        cols_kernel,
        grid_spec=pltpu.PrefetchScalarGridSpec(
            num_scalar_prefetch=1,
            grid=(n // PW,),
            in_specs=[src(d) for d in range(ROWS) for _ in range(2)]
            + [whole] * 3
            + [pl.BlockSpec((8, BLK), lambda i, meta: (0, 0))],
            out_specs=(out, out),
        ),
        out_shape=(jax.ShapeDtypeStruct((2 * PW, n), jnp.bfloat16),) * 2,
        compiler_params=params(),
        cost_estimate=cost(0, 1 << 20),
    )(meta, *[x for pair in pairs for x in pair], w0, l10, w1, tick)


def table_kernel(meta, out):
    for n in range(6 * PB + 8):
        out[n] = jnp.int32(-1)
    for c in range(2):
        base = OWN + 24 * c
        for axis in range(2):
            here = meta[axis]
            for sender in range(ROWS):
                if c == 0:
                    source = jnp.int32(sender)
                elif axis == 0:
                    source = lax.rem(here - sender + ROWS, ROWS)
                else:
                    source = jnp.bitwise_xor(here, sender)
                targets, ranks, places = ranked(meta, base, sender)
                for i in range(CB):

                    @pl.when(targets[i] == here)
                    def _():
                        out[(3 * c + axis) * PB + places[i]] = CAP * source + ranks[i]
                        if c == 1 and axis == 1:
                            out[6 * PB + CAP * source + ranks[i]] = places[i]

        last = jnp.int32(0)
        for p in range(PB):
            slot = out[3 * c * PB + p]
            last = jnp.where(slot >= 0, slot, last)
            out[(3 * c + 2) * PB + p] = last


def tables(meta):
    return pl.pallas_call(
        table_kernel,
        out_shape=jax.ShapeDtypeStruct((6 * PB + 8,), jnp.int32),
        in_specs=[SMEM],
        out_specs=SMEM,
    )(meta)


def trail_kernel(meta, tab, front, xa, y0, y1, y2, y3, low, rh, rl, ch, cl, out):
    p = pl.program_id(0)
    r, s = meta[0], meta[1]
    top = (r == 0) & (p < 4)

    @pl.when(top)
    def _():
        out[...] = jnp.zeros_like(out)

    @pl.when(jnp.logical_not(top))
    def _():
        def mul(a, b):
            return lax.dot_general(a, b, (((1,), (0,)), ((), ())), preferred_element_type=F32)

        for c in range(PB * BLK // PW):
            at = slice(c * PW, (c + 1) * PW)
            prod = mul(rh[...], ch[:, at]) + (mul(rh[...], cl[:, at]) + mul(rl[...], ch[:, at]))
            out[:, at] = front[:, at] - prod

        @pl.when(tab[p] >= 0)
        def _():
            for q in range(PB):
                slot = tab[PB + q]

                @pl.when(slot >= 0)
                def _():
                    at = slice(q * BLK, (q + 1) * BLK)
                    out[:, at] += xa[0, lax.div(slot, 2), 0, lax.rem(slot, 2)]

        @pl.when(tab[3 * PB + p] >= 0)
        def _():
            for m, y in enumerate((y0, y1, y2, y3)):
                for k in range(CAP):
                    q = tab[6 * PB + m * CAP + k]

                    @pl.when(q >= 0)
                    def _():
                        at = pl.ds(pl.multiple_of(q * BLK, BLK), BLK)
                        out[:, at] += y[0, k]

    @pl.when(s == 0)
    def _():
        out[:, : 2 * PW] = low[...]


def trail(meta, tab, front, xa, ys, low, rh, rl, ch, cl):
    n = PB * BLK

    def of_a(p, meta, tab):
        slot = tab[2 * PB + p]
        return (lax.div(slot, 2), 0, lax.rem(slot, 2), 0, 0, 0)

    def of_b(p, meta, tab):
        return (tab[5 * PB + p], 0, 0, 0)

    wide = pl.BlockSpec((BLK, n), lambda p, meta, tab: (p, 0))
    rows = pl.BlockSpec((BLK, 2 * PW), lambda p, meta, tab: (p, 0))
    cols = pl.BlockSpec((2 * PW, n), lambda p, meta, tab: (0, 0))
    return pl.pallas_call(
        trail_kernel,
        grid_spec=pltpu.PrefetchScalarGridSpec(
            num_scalar_prefetch=2,
            grid=(PB,),
            in_specs=[wide, pl.BlockSpec((1, 4, 1, 2, BLK, BLK), of_a)]
            + [pl.BlockSpec((1, CAP, BLK, BLK), of_b)] * 4
            + [rows, rows, rows, cols, cols],
            out_specs=wide,
        ),
        out_shape=jax.ShapeDtypeStruct((n, n), F32),
        compiler_params=params(),
        cost_estimate=cost(0, 1 << 20),
    )(meta, tab, front, xa, *ys, low, rh, rl, ch, cl)


def move(x, axes, fn, sizes, only=None):
    pairs = []
    total = 1
    for size in sizes:
        total *= size

    def unflat(i):
        place = []
        for size in reversed(sizes):
            place.append(i % size)
            i //= size
        return tuple(reversed(place))

    def flat(place):
        i = 0
        for at, size in zip(place, sizes):
            i = i * size + at
        return i

    for i in range(total):
        place = unflat(i)
        if only is None or only(*place):
            pairs.append((i, flat(fn(*place))))
    return lax.ppermute(x, axes if len(axes) > 1 else axes[0], pairs)


def across_cube(x):
    return move(x, ("cube",), lambda g: (g ^ 1,), (8,))


def across_col(x, mask):
    return move(x, ("col",), lambda s: (s ^ mask,), (4,))


def exchange(packed):
    per = packed.shape[0] // 16
    got = lax.all_to_all(packed.reshape(16, per, BLK, BLK), ("row", "col"), 0, 0, tiled=True)
    return got.reshape(4, 4, per // 2, 2, BLK, BLK)


def shards(front_entries, child_update, block_map):
    barrier = lax.optimization_barrier
    front = front_entries[0]
    child = child_update[0]
    row_here, col_here = lax.axis_index("row"), lax.axis_index("col")
    here = jnp.stack([row_here, col_here]).astype(jnp.int32)
    meta = jnp.concatenate([here, block_map.reshape(-1)])
    n = PB * BLK

    sibling = across_cube(child)

    corner = front[: 2 * PW, : 2 * PW]
    corners = [
        move(corner, ("row", "col"), lambda r, s: (d, 0), (4, 4), lambda r, s: r == 0 and s == 0)
        for d in range(1, 4)
    ]
    xa = exchange(pack(meta, child, OWN, meta))

    keep, send = strips(meta, child, sibling)
    got = across_col(send, 1)
    got, *rows = barrier((got, *row_pack(meta, sibling, OWN + 24)))
    chosen = choose(meta, keep, got)
    far = across_col(chosen, 2)
    corner, corners, _ = barrier((corner, corners, chosen))
    corner = jnp.where(row_here == 0, corner, corners[0] + corners[1] + corners[2])
    wide = jnp.concatenate([front[:, : 2 * PW], corner], axis=0)
    fs = [wide[:, q * BLK : (q + 1) * BLK] for q in range(4)]
    fs = [fs[0]] + [
        move(fs[q], ("col",), lambda s: (q,), (4,), lambda s: s == 0) for q in range(1, 4)
    ]
    rows = [rows[0]] + [
        move(rows[d], ("row",), lambda r: ((r + d) % 4,), (4,)) for d in range(1, 4)
    ]
    tab = tables(meta)
    xa, far, tab, *rows = barrier((xa, far, tab, *rows))
    outs = band(meta, keep, got, far)
    xs = [outs[0]] + [
        move(outs[d], ("row",), lambda r: ((r + d) % 4,), (4,)) for d in range(1, 4)
    ]
    mine = strip_add(meta, fs, xs)

    far = across_col(mine, 2)
    mine, *rows = barrier((mine, *rows))
    cols = col_pack(meta, rows, OWN + 24)
    mine, far, *cols = barrier((mine, far, *cols))
    own = jnp.stack([mine, far])
    other = across_col(own, 1)
    ys = [cols[0]] + [across_col(cols[m], m) for m in range(1, 4)]

    def step(x, start, stop):
        return move(
            x,
            ("row", "col"),
            lambda r, s: ((s + stop) % 4, s),
            (4, 4),
            lambda r, s: r == (s + start) % 4,
        )

    own_band, other_band = own[:, :n], other[:, :n]
    o1, o3 = step(own_band, 0, 1), step(own_band, 0, 3)
    g1, g3 = step(other_band, 0, 1), step(other_band, 0, 3)
    w0, l10, w1, tick = factor(meta, own, other)
    tick = across_col(tick, 1)
    o1, o3, g1, g3, w1, tick, ys[1], ys[2] = barrier((o1, o3, g1, g3, w1, tick, ys[1], ys[2]))
    o2, g2 = step(o1, 1, 2), step(g3, 3, 2)
    low, rh, rl, tick = factor_rows(meta, own, other, w0, l10, w1, tick)
    tick = across_col(tick, 1)
    tick, o2, g2, ys[3] = barrier((tick, o2, g2, ys[3]))
    ch, cl = factor_cols(
        meta, ((own, other), (o1, g1), (o2, g2), (o3, g3)), w0, l10, w1, tick
    )
    return trail(meta, tab, front, xa, ys, low, rh, rl, ch, cl)[None]


def solution(mesh):
    in_specs = (P("cube", "row", "col"), P("cube", "row", "col"), P("cube", None, None))
    out_specs = P("cube", "row", "col")
    return jax.shard_map(shards, mesh=mesh, in_specs=in_specs, out_specs=out_specs, check_vma=False)
```
